32 devices in a mesh: group: 2 (over y), node: 8 (over z, x), tp: 2 (over core).
Axes of the slice: x: 2, y: 2, z: 4, core: 2. Of those that a mesh axis runs over, the one named last changes fastest.
Arguments:
- residual: bfloat16 [256, 6144], P(('group', 'node'), 'tp'), parts along dimension 0, may hold values from -70 to 70
- queries: bfloat16 [256, 6144], P(('group', 'node'), 'tp'), parts along dimension 0, may hold values from -150 to 150
- new_keys: bfloat16 [256, 1024], P(('group', 'node'), 'tp'), parts along dimension 0, may hold values from -5 to 5
- new_values: bfloat16 [256, 1024], P(('group', 'node'), 'tp'), parts along dimension 0, may hold values from -6 to 6
- cache_keys: bfloat16 [256, 8, 96, 128], P(('group', 'node'), 'tp'), parts along dimension 0, may hold values from -5 to 5
- cache_values: bfloat16 [256, 8, 96, 128], P(('group', 'node'), 'tp'), parts along dimension 0, may hold values from -6 to 6
- lengths: int32 [256], P(('group', 'node')), parts along dimension 0, may hold values from 1 to 96, as said below
- routes: int32 [256, 2], P(('group', 'node')), parts along dimension 0, may hold values from 0 to 3, all different within a row; in each aligned block of 16 rows (0 to 15, 16 to 31, ...) at most 9 rows name the same one
- norm_gain: float32 [6144], P('tp'), may hold values from 0.1 to 1.9
- router_weight: bfloat16 [6144, 4], P('tp'), may hold values from -0.078125 to 0.078125
- gate_weight: bfloat16 [6144, 32768], P('tp', 'node'), may hold values from -0.078125 to 0.078125
- up_weight: bfloat16 [6144, 32768], P('tp', 'node'), may hold values from -0.078125 to 0.078125
- down_weight: bfloat16 [32768, 6144], P('node', 'tp'), may hold values from -0.0625 to 0.0625
Outputs:
- mixed: bfloat16 [256, 6144], P(('group', 'node'), 'tp'), parts along dimension 0
The draws below stay inside these ranges and needn't reach their ends.
There are 2 independent parts, one for each index of `group`. The reference program is written for one: setup_inputs(seed, part) draws one part's arguments, and reference() takes and returns one part's arrays. A program takes and returns all parts, laid end to end along the dimension named above; an argument that names none is the same for every part. Nothing has to cross between parts.
Inputs may be any that keep to these rules, and one draw needn't show every extreme that they name: `routes`: each row names two different experts; within each aligned block of 16 rows (the rows of one node index) no expert is named by more than 9 rows. `lengths`: some row's cache is full.
All inputs are finite; a program needn't handle non-finite values.
Results may differ from the reference program's by a relative error of at most 0.005.
Values may be sent and summed in bfloat16 or wider, within the bound.
A program may use at most 192 MiB of HBM per device.

```python
import math
import jax
import jax.numpy as jnp
import numpy as np
from jax import lax

D = 6144
HEADS = 48
KV_HEADS = 8
HEAD_DIM = 128
EXPERTS = 4
FF = 8192
TOK_DEV = 16
CACHE = 96
SLOTS = 9
ROWS = 128
N_NODE = 8


def shared_anchor(key):
    return jnp.clip(jax.random.normal(key, (ROWS, KV_HEADS, HEAD_DIM), jnp.float32), -5.0, 5.0)


def draw_new_keys(key, part):
    anchor = shared_anchor(key)
    return anchor.reshape(ROWS, KV_HEADS * HEAD_DIM).astype(jnp.bfloat16)


def draw_queries(key, part):
    key = jax.random.fold_in(key, 3)
    noise = jnp.clip(jax.random.normal(key, (ROWS, HEADS, HEAD_DIM), jnp.float32), -6.0, 6.0)
    return noise.reshape(ROWS, HEADS * HEAD_DIM).astype(jnp.bfloat16)


def draw_cache_keys(key, part):
    key = jax.random.fold_in(key, 7)
    entries = jnp.clip(jax.random.normal(key, (ROWS, KV_HEADS, CACHE, HEAD_DIM), jnp.float32), -5.0, 5.0)
    return entries.astype(jnp.bfloat16)


def draw_lengths(key, part):
    key = jax.random.fold_in(key, 11)
    first_key, second_key, third_key = jax.random.split(key, 3)
    drawn = jax.random.randint(first_key, (ROWS,), 1, CACHE + 1)
    shrink = jax.random.randint(second_key, (ROWS,), 1, 5)
    drawn = jnp.maximum(1, drawn * shrink // 4)
    longest = jax.random.randint(third_key, (), 0, ROWS)
    return drawn.at[longest].set(CACHE).astype(jnp.int32)


def draw_residual(key, part):
    key = jax.random.fold_in(key, 13)
    noise_key, row_key, column_key = jax.random.split(key, 3)
    noise = jnp.clip(jax.random.normal(noise_key, (ROWS, D), jnp.float32), -6.0, 6.0)
    row_scale = jnp.exp(jax.random.uniform(row_key, (ROWS, 1), jnp.float32, math.log(0.3), math.log(3.0)))
    column_scale = jnp.exp(jax.random.uniform(column_key, (1, D), jnp.float32, math.log(0.3), math.log(3.0)))
    return (noise * row_scale * column_scale).astype(jnp.bfloat16)


def block_scale(stream_key, dims, cuts, smallest, high):
    def one(axis_at, parts):
        heights = jax.random.uniform(jax.random.fold_in(jax.random.fold_in(stream_key, 6), axis_at), (parts,), jnp.float32, smallest / len(cuts), high / len(cuts))
        return jnp.repeat(jnp.exp(heights), dims[axis_at] // parts).reshape((-1,) + (1,) * (len(dims) - axis_at - 1))

    level = one(*cuts[0])
    for cut in cuts[1:]:
        level = level * one(*cut)
    return level


def assign_block(stream_key, own, number, rows, number_of, top, limit, lean):
    order = jax.random.permutation(stream_key, number_of)
    heavy_load, common = shares(number_of, rows * top, limit, lean, True), shares(number_of, rows * top, limit, lean, False)
    places = jnp.arange(number_of)

    def named(sizes, offset_by):
        used = int((sizes > 0).sum())
        fixed = max(1, used // 4)
        moved = fixed + (places - fixed + offset_by * (used - fixed)) % max(1, number_of - fixed)
        return jnp.zeros((number_of,), jnp.int32).at[order[jnp.where(places < fixed, places, moved)]].set(jnp.asarray(sizes, jnp.int32))

    sizes = jnp.where(number % 4 == 0, named(heavy_load, number // 4), named(common, number - number // 4 - 1))
    mixed = jax.random.permutation(jax.random.fold_in(own, 3), number_of)
    donor, taker = mixed[0:number_of // 2 * 2:2], mixed[1:number_of // 2 * 2:2]
    slack = jnp.minimum(sizes[donor] - 1, limit - sizes[taker]) // 2
    slack = jnp.where((donor == order[0]) | (taker == order[0]) | (sizes[taker] == 0), 0, jnp.maximum(slack, 0))
    moved = jax.random.randint(jax.random.fold_in(own, 4), (number_of // 2,), 0, 1 << 20) % (slack + 1)
    sizes = sizes.at[donor].add(-moved).at[taker].add(moved)
    items = jnp.searchsorted(jnp.cumsum(sizes), jnp.arange(rows * top), side="right").astype(jnp.int32)
    grid = items.reshape(top, rows).T
    grid = grid[jax.random.permutation(jax.random.fold_in(own, 1), rows)]
    offset_by = jax.random.randint(jax.random.fold_in(own, 2), (rows, 1), 0, top)
    return jnp.take_along_axis(grid, (jnp.arange(top)[None, :] + offset_by) % top, axis=1)


def shares(count, total, limit, skew, full):
    weights = [(1 << 20) // math.isqrt(standing ** skew) + 1 for standing in range(1, count + 1)]
    largest = limit if full else min(limit, max(-(-total // count), total * weights[0] // sum(weights)))
    least = 1 if total - largest >= count - 1 else 0
    holding, rest = [largest] + [least] * (count - 1), total - largest - least * (count - 1)
    while rest > 0:
        candidates = [i for i in range(1, count) if holding[i] < largest] or [i for i in range(1, count) if holding[i] < limit]
        pool, budget = sum([weights[i] for i in candidates]), rest
        for i in candidates:
            extra = min(limit - holding[i], max(1, budget * weights[i] // pool), rest)
            holding[i] = holding[i] + extra
            rest = rest - extra
    return np.array(holding)


def scatter_about(key, extent, scale, most, cuts=(), kind=jnp.bfloat16):
    gain = block_scale(key, extent, cuts, -0.22, 0.18) if cuts else 1.0
    values = jax.random.normal(key, extent, jnp.float32) * scale * gain
    return jnp.minimum(jnp.maximum(values, -most), most).astype(kind)


def setup_inputs(seed: int = 0, part: int = 0) -> dict:
    keys = jax.random.split(jax.random.key(seed), 14)
    own_keys = jax.random.split(jax.random.fold_in(keys[13], part), 14)
    residual = draw_residual(jax.random.fold_in(jax.random.fold_in(keys[13], part), 71), part)
    queries = draw_queries(jax.random.fold_in(jax.random.fold_in(keys[13], part), 71), part)
    new_keys = draw_new_keys(jax.random.fold_in(jax.random.fold_in(keys[13], part), 71), part)
    new_values = scatter_about(own_keys[3], (ROWS, KV_HEADS * HEAD_DIM), 1.0, 6.0, ((0, 8), (1, 2)))
    cache_keys = draw_cache_keys(jax.random.fold_in(jax.random.fold_in(keys[13], part), 71), part)
    cache_values = scatter_about(own_keys[5], (ROWS, KV_HEADS, CACHE, HEAD_DIM), 1.0, 6.0, ((0, 8), (1, 2)))
    lengths = draw_lengths(jax.random.fold_in(jax.random.fold_in(keys[13], part), 71), part)
    routes_keys = jax.random.split(jax.random.fold_in(own_keys[7], 1), ROWS // TOK_DEV)
    routes_turns = jax.random.permutation(jax.random.fold_in(own_keys[7], 3), ROWS // TOK_DEV)
    routes = jax.vmap(lambda own, number: assign_block(jax.random.fold_in(own_keys[7], 2), own, number, TOK_DEV, EXPERTS, 2, SLOTS, 1))(routes_keys, routes_turns).reshape((ROWS, 2))
    norm_gain = jnp.clip(1.0 + 0.18 * jax.random.normal(keys[8], (D,), jnp.float32), 0.1, 1.9)
    router_weight = scatter_about(keys[9], (D, EXPERTS), D ** -0.5, 0.078125, ((0, 2),))
    gate_weight = scatter_about(keys[10], (D, EXPERTS * FF), D ** -0.5, 0.078125, ((0, 2), (1, 8)))
    up_weight = scatter_about(keys[11], (D, EXPERTS * FF), D ** -0.5, 0.078125, ((0, 2), (1, 8)))
    down_weight = scatter_about(keys[12], (EXPERTS * FF, D), FF ** -0.5, 0.0625, ((0, 8), (1, 2)))
    return dict(residual=residual, queries=queries, new_keys=new_keys, new_values=new_values, cache_keys=cache_keys, cache_values=cache_values, lengths=lengths, routes=routes, norm_gain=norm_gain, router_weight=router_weight, gate_weight=gate_weight, up_weight=up_weight, down_weight=down_weight)


def attention_rows(queries, new_keys, new_values, cache_keys, cache_values, lengths):
    row_count, kv_count, cache_len, head_dim = cache_keys.shape
    query_grid = queries.reshape(row_count, kv_count, -1, head_dim).astype(jnp.float32)
    factor = 1.0 / math.sqrt(head_dim)
    scores = jnp.einsum('rkgd,rkld->rkgl', query_grid, cache_keys.astype(jnp.float32)) * factor
    position = lax.broadcasted_iota(jnp.int32, (1, 1, 1, cache_len), 3)
    scores = jnp.where(position < lengths[:, None, None, None], scores, -jnp.inf)
    own_key = new_keys.reshape(row_count, kv_count, head_dim).astype(jnp.float32)
    own_score = jnp.einsum('rkgd,rkd->rkg', query_grid, own_key) * factor
    highest = jnp.maximum(lax.optimization_barrier(jnp.max(scores, axis=3)), own_score)
    weights = jnp.exp(scores - highest[..., None])
    own_weight = jnp.exp(own_score - highest)
    denominator = lax.optimization_barrier(jnp.sum(weights, axis=3)) + own_weight
    attn_probs = (weights / denominator[..., None]).astype(jnp.bfloat16)
    own_prob = (own_weight / denominator).astype(jnp.bfloat16)
    attended = jnp.einsum('rkgl,rkld->rkgd', attn_probs.astype(jnp.float32), cache_values.astype(jnp.float32))
    own_value = new_values.reshape(row_count, kv_count, 1, head_dim).astype(jnp.float32)
    attended = attended + own_prob.astype(jnp.float32)[..., None] * own_value
    return attended.reshape(row_count, -1)

def reference(residual, queries, new_keys, new_values, cache_keys, cache_values, lengths, routes, norm_gain, router_weight, gate_weight, up_weight, down_weight):
    attended = attention_rows(queries, new_keys, new_values, cache_keys, cache_values, lengths)
    mixed_in = residual.astype(jnp.float32) + attended
    mean_square = lax.optimization_barrier(jnp.mean(mixed_in * mixed_in, axis=1))
    normed = (mixed_in * lax.rsqrt(mean_square + 1e-05)[:, None] * norm_gain).astype(jnp.bfloat16)
    logits = jnp.dot(normed, router_weight, preferred_element_type=jnp.float32)
    picked = jnp.take_along_axis(logits, routes, axis=1)
    first_weight = jax.nn.sigmoid(picked[:, 0] - picked[:, 1])
    second_weight = jax.nn.sigmoid(picked[:, 1] - picked[:, 0])
    row_count, model_width = normed.shape
    expert_count = router_weight.shape[1]
    hidden_units = gate_weight.shape[1] // expert_count
    per_expert = N_NODE // expert_count
    piece_units = hidden_units // per_expert
    gate_stack = gate_weight.reshape(model_width, expert_count, hidden_units).transpose(1, 0, 2)
    up_stack = up_weight.reshape(model_width, expert_count, hidden_units).transpose(1, 0, 2)
    down_stack = down_weight.reshape(expert_count, per_expert, piece_units, model_width)

    def expert_step(running, inputs):
        gate_part, up_part, down_part, expert_index = inputs
        gate_value = jnp.dot(normed, gate_part, preferred_element_type=jnp.float32)
        up_value = jnp.dot(normed, up_part, preferred_element_type=jnp.float32)
        hidden = (jax.nn.silu(gate_value) * up_value).astype(jnp.bfloat16)
        hidden_pieces = hidden.reshape(row_count, per_expert, piece_units).transpose(1, 0, 2)

        def piece_step(accumulated, paired):
            hidden_piece, down_piece = paired
            piece_term = jnp.dot(hidden_piece, down_piece, preferred_element_type=jnp.float32).astype(jnp.bfloat16)
            piece_term = lax.optimization_barrier(piece_term)
            return (accumulated + piece_term.astype(jnp.float32), None)
        output = lax.scan(piece_step, jnp.zeros((row_count, model_width), jnp.float32), (hidden_pieces, down_part))[0]
        mixing = jnp.where(routes[:, 0] == expert_index, first_weight, 0.0) + jnp.where(routes[:, 1] == expert_index, second_weight, 0.0)
        return (running + mixing[:, None] * output, None)
    expert_sum = lax.scan(expert_step, jnp.zeros((row_count, model_width), jnp.float32), (gate_stack, up_stack, down_stack, jnp.arange(expert_count, dtype=jnp.int32)))[0]
    return (mixed_in + expert_sum).astype(jnp.bfloat16)
```

```python
import functools
import math

import jax
import jax.numpy as jnp
from jax import lax
from jax.experimental import pallas as pl
from jax.experimental.pallas import tpu as pltpu
from jax.sharding import PartitionSpec as P

F32, BF16 = jnp.float32, jnp.bfloat16
NT = (((1,), (1,)), ((), ()))
SLOT_MAX = 48
CW = 512


def layer_kernel(
    cfg,
    lens_ref,
    routes_ref,
    res_ref,
    q_ref,
    nk_ref,
    nv_ref,
    ck_hbm,
    cv_hbm,
    gain_ref,
    router_ref,
    gate_hbm,
    up_hbm,
    down_hbm,
    out_ref,
    kbuf,
    vbuf,
    wbuf,
    xbuf,
    mixed,
    stat_s,
    stat_r,
    own_part,
    psend,
    precv,
    hidden,
    xsend,
    xrecv,
    xown,
    zsend,
    zrecv,
    zown,
    cache_sem,
    wsem,
    stat_sem,
    dsend_sem,
    drecv_sem,
    psend_sem,
    precv_sem,
    xsend_sem,
    xrecv_sem,
    zsend_sem,
    zrecv_sem,
):
    A, B, R, W, FF, KV, L, H = cfg
    N, M = A * B, A * B * R
    HQ = W // (KV * H)
    KB = min(1024, FF)
    nc, nk = FF // CW, W // 1024
    nj, nd = W // CW, FF // KB
    direct = nc * nk * 2 + nj * nd <= SLOT_MAX
    node = lax.axis_index("node")
    tp = lax.axis_index("tp")
    a_me, b_me = lax.div(node, B), lax.rem(node, B)
    mine = b_me * A + a_me

    def outer(i):
        return lax.rem(a_me + i, A)

    def inner(i):
        return lax.rem(b_me + i, B)

    def dev(a, b):
        return {"node": a * B + b}

    def gu_copy(c, w, k):
        slot = (c * 2 + w) * nk + k
        src = gate_hbm if w == 0 else up_hbm
        col = pl.multiple_of(c * CW, CW)
        return pltpu.make_async_copy(
            src.at[pl.ds(k * 1024, 1024), pl.ds(col, CW)], wbuf.at[slot], wsem.at[slot]
        )

    def down_slot(j, k):
        return j * nd + k + (nc * nk * 2 if direct else 0)

    def down_copy(j, k):
        slot = down_slot(j, k)
        col = pl.multiple_of(j * CW, CW)
        return pltpu.make_async_copy(
            down_hbm.at[pl.ds(k * KB, KB), pl.ds(col, CW)],
            wbuf.at[slot, pl.ds(0, KB)],
            wsem.at[slot],
        )

    kcopy = pltpu.make_async_copy(ck_hbm, kbuf, cache_sem.at[0])
    vcopy = pltpu.make_async_copy(cv_hbm, vbuf, cache_sem.at[1])
    kcopy.start()
    vcopy.start()

    @pl.loop(0, nc)
    def _(c):
        for w in range(2):
            for k in range(nk):
                gu_copy(c, w, k).start()

    if direct:

        @pl.loop(0, nj)
        def _(j):
            for k in range(nd):
                down_copy(j, k).start()

    barrier = pltpu.get_barrier_semaphore()
    pl.semaphore_signal(
        barrier, inc=1, device_id={"tp": 1 - tp}, device_id_type=pl.DeviceIdType.MESH
    )
    for i in range(1, A):
        pl.semaphore_signal(
            barrier, inc=1, device_id=dev(outer(i), b_me), device_id_type=pl.DeviceIdType.MESH
        )
    for i in range(1, B):
        pl.semaphore_signal(
            barrier, inc=1, device_id=dev(a_me, inner(i)), device_id_type=pl.DeviceIdType.MESH
        )

    kcopy.wait()
    vcopy.wait()
    factor = 1.0 / math.sqrt(H)
    row128 = lax.broadcasted_iota(jnp.int32, (R, 128), 0)
    lenv = jnp.zeros((R, 128), jnp.int32)
    r0 = jnp.zeros((R, 128), jnp.int32)
    r1 = jnp.zeros((R, 128), jnp.int32)
    for r in range(R):
        lenv = jnp.where(row128 == r, lens_ref[r], lenv)
        r0 = jnp.where(row128 == r, routes_ref[0, r], r0)
        r1 = jnp.where(row128 == r, routes_ref[1, r], r1)
    col = lax.broadcasted_iota(jnp.int32, (R, R * L), 1)
    row = lax.broadcasted_iota(jnp.int32, (R, R * L), 0)
    valid = jnp.logical_and(col >= row * L, col < row * L + lenv[:, 0:1])
    bias = jnp.where(valid, 0.0, -jnp.inf).astype(F32)
    bias = jnp.concatenate([bias] * HQ, axis=0)
    square = jnp.zeros((R, 1), F32)
    logits = jnp.zeros((R, router_ref.shape[0]), F32)
    for g in range(KV):
        base = g * HQ * H
        q = jnp.concatenate([q_ref[:, base + h * H : base + (h + 1) * H] for h in range(HQ)], axis=0)
        keys = kbuf[:, g].reshape(R * L, H)
        values = vbuf[:, g].reshape(R * L, H)
        scores = lax.dot_general(q, keys, NT, preferred_element_type=F32) * factor + bias
        own_key = jnp.concatenate([nk_ref[:, g * H : (g + 1) * H].astype(F32)] * HQ, axis=0)
        own = jnp.sum(q.astype(F32) * own_key, axis=1, keepdims=True) * factor
        highest = jnp.maximum(jnp.max(scores, axis=1, keepdims=True), own)
        weights = jnp.exp(scores - highest)
        own_weight = jnp.exp(own - highest)
        total = jnp.sum(weights, axis=1, keepdims=True) + own_weight
        probs = (weights / total).astype(BF16)
        own_prob = (own_weight / total).astype(BF16).astype(F32)
        attended = jnp.dot(probs, values, preferred_element_type=F32)
        own_value = jnp.concatenate([nv_ref[:, g * H : (g + 1) * H].astype(F32)] * HQ, axis=0)
        attended = attended + own_prob * own_value
        for h in range(HQ):
            lo = base + h * H
            m = res_ref[:, lo : lo + H].astype(F32) + attended[h * R : (h + 1) * R]
            mixed[:, lo : lo + H] = m
            square = square + jnp.sum(m * m, axis=1, keepdims=True)
    gained = (mixed[...] * gain_ref[...]).astype(BF16)
    logits = lax.dot_general(gained, router_ref[...], NT, preferred_element_type=F32)
    stat_s[...] = jnp.zeros_like(stat_s)
    stat_s[:, 0:A] = logits
    stat_s[:, A : A + 1] = square

    pl.semaphore_wait(barrier, 1 + (A - 1) + (B - 1))
    stat_copy = pltpu.make_async_remote_copy(
        stat_s,
        stat_r,
        stat_sem.at[0],
        stat_sem.at[1],
        device_id={"tp": 1 - tp},
        device_id_type=pl.DeviceIdType.MESH,
    )
    stat_copy.start()
    stat_copy.wait()
    stat = stat_s[...] + stat_r[...]
    inverse = lax.rsqrt(stat[:, A : A + 1] / (2 * W) + 1e-05)
    logit = stat * inverse
    lane = lax.broadcasted_iota(jnp.int32, (R, 128), 1)
    p0 = jnp.sum(jnp.where(lane == r0, logit, 0.0), axis=1, keepdims=True)
    p1 = jnp.sum(jnp.where(lane == r1, logit, 0.0), axis=1, keepdims=True)
    w0 = 1.0 / (1.0 + jnp.exp(p1 - p0))
    w1 = 1.0 / (1.0 + jnp.exp(p0 - p1))
    pair = jnp.where(lane == r0, w0, 0.0) + jnp.where(lane == r1, w1, 0.0)
    pair_hi = pair.astype(BF16)
    lane_lo = lane - A
    low = jnp.where(lane_lo == r0, w0, 0.0) + jnp.where(lane_lo == r1, w1, 0.0)
    low = (low - low.astype(BF16).astype(F32)).astype(BF16)
    xbuf[mine, :, W : W + 128] = pair_hi + low
    xbuf[mine, :, 0:W] = (mixed[...] * inverse * gain_ref[...]).astype(BF16)

    def x_copy(block, sem, a, b):
        return pltpu.make_async_remote_copy(
            xbuf.at[block],
            xbuf.at[block],
            dsend_sem.at[sem],
            drecv_sem.at[block],
            device_id=dev(a, b),
            device_id_type=pl.DeviceIdType.MESH,
        )

    def z_send(i):
        return x_copy(mine, b_me * A + outer(i), outer(i), b_me)

    def relay(i, t):
        return x_copy(b_me * A + outer(i), inner(t) * A + outer(i), a_me, inner(t))

    def arrival(i, t):
        return x_copy(inner(t) * A + outer(i), 0, a_me, inner(1))

    for i in range(1, A):
        z_send(i).start()
    for t in range(1, B):
        relay(0, t).start()
    for i in range(1, A):
        arrival(i, 0).wait_recv()
        for t in range(1, B):
            relay(i, t).start()
    for t in range(1, B):
        for i in range(A):
            arrival(i, t).wait_recv()

    def part_copy(c):
        s = lax.rem(c, 2)
        return pltpu.make_async_remote_copy(
            psend.at[s],
            precv.at[c],
            psend_sem.at[s],
            precv_sem.at[c],
            device_id={"tp": 1 - tp},
            device_id_type=pl.DeviceIdType.MESH,
        )

    def finish(c):
        s = lax.rem(c, 2)
        part_copy(c).wait_recv()
        gate = own_part[s, 0] + precv[c, 0].astype(F32)
        up = own_part[s, 1] + precv[c, 1].astype(F32)
        value = (gate / (1.0 + jnp.exp(-gate)) * up).astype(BF16)
        hidden[:, pl.ds(pl.multiple_of(c * CW, CW), CW)] = value

    @pl.loop(0, nc)
    def _(c):
        s = lax.rem(c, 2)

        @pl.when(c >= 2)
        def _():
            part_copy(c - 2).wait_send()

        for w in range(2):
            acc = None
            for k in range(nk):
                gu_copy(c, w, k).wait()
                lhs = xbuf[:, :, k * 1024 : (k + 1) * 1024].reshape(M, 1024)
                term = jnp.dot(lhs, wbuf[(c * 2 + w) * nk + k], preferred_element_type=F32)
                acc = term if acc is None else acc + term
            own_part[s, w] = acc
            psend[s, w] = acc.astype(BF16)
        part_copy(c).start()
        if not direct:
            per = 2 * nk // nd if (2 * nk) % nd == 0 else 1

            @pl.when(c * per < nj)
            def _():
                for p in range(per):

                    @pl.when(c * per + p < nj)
                    def _():
                        for k in range(nd):
                            down_copy(c * per + p, k).start()

        @pl.when(c >= 1)
        def _():
            finish(c - 1)

    finish(nc - 1)
    for c in range(max(0, nc - 2), nc):
        part_copy(c).wait_send()

    side = xbuf[:, :, W : W + 128].reshape(M, 128).astype(F32)
    lane_m = lax.broadcasted_iota(jnp.int32, (M, 128), 1)
    keep = jnp.logical_or(lane_m == a_me, lane_m == a_me + A)
    pairw = jnp.sum(jnp.where(keep, side, 0.0), axis=1, keepdims=True)

    G = A * R

    def xs_copy(j, t):
        other = inner(t)
        return pltpu.make_async_remote_copy(
            xsend.at[j, other],
            xrecv.at[j, b_me],
            xsend_sem.at[j, other],
            xrecv_sem.at[j, b_me],
            device_id=dev(a_me, other),
            device_id_type=pl.DeviceIdType.MESH,
        )

    def xs_arrival(j, t):
        other = inner(t)
        return pltpu.make_async_remote_copy(
            xsend.at[j, b_me],
            xrecv.at[j, other],
            xsend_sem.at[j, b_me],
            xrecv_sem.at[j, other],
            device_id=dev(a_me, other),
            device_id_type=pl.DeviceIdType.MESH,
        )

    def zs_copy(j, i):
        other = outer(i)
        return pltpu.make_async_remote_copy(
            zsend.at[j, other],
            zrecv.at[j, a_me],
            zsend_sem.at[j, other],
            zrecv_sem.at[j, a_me],
            device_id=dev(other, b_me),
            device_id_type=pl.DeviceIdType.MESH,
        )

    def zs_arrival(j, i):
        other = outer(i)
        return pltpu.make_async_remote_copy(
            zsend.at[j, a_me],
            zrecv.at[j, other],
            zsend_sem.at[j, a_me],
            zrecv_sem.at[j, other],
            device_id=dev(other, b_me),
            device_id_type=pl.DeviceIdType.MESH,
        )

    def stage_one(j):
        acc = None
        for k in range(nd):
            down_copy(j, k).wait()
            term = jnp.dot(
                hidden[:, k * KB : (k + 1) * KB],
                wbuf[down_slot(j, k), 0:KB],
                preferred_element_type=F32,
            )
            acc = term if acc is None else acc + term
        acc = acc * pairw
        for b in range(B):
            xsend[j, b] = acc[b * G : (b + 1) * G].astype(BF16)
            mask = jnp.where(b_me == b, 1.0, 0.0)
            if b == 0:
                kept = acc[0:G] * mask
            else:
                kept = kept + acc[b * G : (b + 1) * G] * mask
        xown[lax.rem(j, 2)] = kept
        for t in range(1, B):
            xs_copy(j, t).start()

    def stage_two(j):
        total = xown[lax.rem(j, 2)]
        for t in range(1, B):
            xs_arrival(j, t).wait_recv()
            total = total + xrecv[j, inner(t)].astype(F32)
        zown[j] = total
        for a in range(A):
            zsend[j, a] = total[a * R : (a + 1) * R].astype(BF16)
        for i in range(1, A):
            zs_copy(j, i).start()

    def stage_three(j):
        cols = pl.ds(pl.multiple_of(j * CW, CW), CW)
        total = mixed[:, cols] + zown[j, pl.ds(pl.multiple_of(a_me * R, R), R), :]
        for i in range(1, A):
            zs_arrival(j, i).wait_recv()
            total = total + zrecv[j, outer(i)].astype(F32)
        out_ref[:, cols] = total.astype(BF16)

    @pl.loop(0, nj)
    def _(j):
        stage_one(j)

        @pl.when(j >= 1)
        def _():
            stage_two(j - 1)

        @pl.when(j >= 2)
        def _():
            stage_three(j - 2)

    stage_two(nj - 1)
    stage_three(nj - 2)
    stage_three(nj - 1)

    for i in range(1, A):
        z_send(i).wait_send()
    for t in range(1, B):
        for i in range(A):
            relay(i, t).wait_send()

    @pl.loop(0, nj)
    def _(j):
        for t in range(1, B):
            xs_copy(j, t).wait_send()
        for i in range(1, A):
            zs_copy(j, i).wait_send()


def local(
    residual,
    queries,
    new_keys,
    new_values,
    cache_keys,
    cache_values,
    lengths,
    routes,
    norm_gain,
    router_weight,
    gate_weight,
    up_weight,
    down_weight,
):
    R, W = residual.shape
    FF = gate_weight.shape[1]
    _, KV, L, H = cache_keys.shape
    A = router_weight.shape[1]
    B = lax.axis_size("node") // A
    N, M = A * B, A * B * R
    KB = min(1024, FF)
    nc, nk, nj, nd = FF // CW, W // 1024, W // CW, FF // KB
    gu = nc * nk * 2
    slots = gu + nj * nd if gu + nj * nd <= SLOT_MAX else gu
    cfg = (A, B, R, W, FF, KV, L, H)
    vmem = pl.BlockSpec(memory_space=pltpu.VMEM)
    smem = pl.BlockSpec(memory_space=pltpu.SMEM)
    hbm = pl.BlockSpec(memory_space=pl.ANY)
    dma = pltpu.SemaphoreType.DMA
    return pl.pallas_call(
        functools.partial(layer_kernel, cfg),
        out_shape=jax.ShapeDtypeStruct((R, W), BF16),
        in_specs=[smem, smem, vmem, vmem, vmem, vmem, hbm, hbm, vmem, vmem, hbm, hbm, hbm],
        out_specs=vmem,
        scratch_shapes=[
            pltpu.VMEM((R, KV, L, H), BF16),
            pltpu.VMEM((R, KV, L, H), BF16),
            pltpu.VMEM((slots, 1024, CW), BF16),
            pltpu.VMEM((N, R, W + 128), BF16),
            pltpu.VMEM((R, W), F32),
            pltpu.VMEM((R, 128), F32),
            pltpu.VMEM((R, 128), F32),
            pltpu.VMEM((2, 2, M, CW), F32),
            pltpu.VMEM((2, 2, M, CW), BF16),
            pltpu.VMEM((nc, 2, M, CW), BF16),
            pltpu.VMEM((M, FF), BF16),
            pltpu.VMEM((nj, B, A * R, CW), BF16),
            pltpu.VMEM((nj, B, A * R, CW), BF16),
            pltpu.VMEM((2, A * R, CW), F32),
            pltpu.VMEM((nj, A, R, CW), BF16),
            pltpu.VMEM((nj, A, R, CW), BF16),
            pltpu.VMEM((nj, A * R, CW), F32),
            dma((2,)),
            dma((slots,)),
            dma((2,)),
            dma((N,)),
            dma((N,)),
            dma((2,)),
            dma((nc,)),
            dma((nj, B)),
            dma((nj, B)),
            dma((nj, A)),
            dma((nj, A)),
        ],
        compiler_params=pltpu.CompilerParams(
            collective_id=0, has_side_effects=True, vmem_limit_bytes=63 * 1024 * 1024
        ),
    )(
        lengths,
        routes.T,
        residual,
        queries,
        new_keys,
        new_values,
        cache_keys,
        cache_values,
        norm_gain.reshape(1, -1),
        router_weight.T,
        gate_weight,
        up_weight,
        down_weight,
    )


def solution(mesh):
    placed = (
        P(("group", "node"), "tp"),
        P(("group", "node"), "tp"),
        P(("group", "node"), "tp"),
        P(("group", "node"), "tp"),
        P(("group", "node"), "tp", None, None),
        P(("group", "node"), "tp", None, None),
        P(("group", "node")),
        P(("group", "node"), None),
        P("tp"),
        P("tp", None),
        P("tp", "node"),
        P("tp", "node"),
        P("node", "tp"),
    )
    return jax.shard_map(
        local, mesh=mesh, in_specs=placed, out_specs=P(("group", "node"), "tp"), check_vma=False
    )
```

```python
import functools
import math

import jax
import jax.numpy as jnp
from jax import lax
from jax.experimental import pallas as pl
from jax.experimental.pallas import tpu as pltpu
from jax.sharding import PartitionSpec as P

F32, BF16 = jnp.float32, jnp.bfloat16
NT = (((1,), (1,)), ((), ()))
SLOT_MAX = 48
CW = 512


def layer_kernel(
    cfg,
    lens_ref,
    routes_ref,
    res_ref,
    q_ref,
    nk_ref,
    nv_ref,
    ck_hbm,
    cv_hbm,
    gain_ref,
    router_ref,
    gate_hbm,
    up_hbm,
    down_hbm,
    out_ref,
    kbuf,
    vbuf,
    wbuf,
    xbuf,
    side_buf,
    mixed,
    stat_s,
    stat_r,
    own_part,
    psend,
    precv,
    hidden,
    xsend,
    xrecv,
    xown,
    zsend,
    zrecv,
    zown,
    cache_sem,
    wsem,
    stat_sem,
    dsend_sem,
    rsend_sem,
    drecv_sem,
    psend_sem,
    precv_sem,
    xsend_sem,
    xrecv_sem,
    zsend_sem,
    zrecv_sem,
):
    A, B, R, W, FF, KV, L, H = cfg
    N, M = A * B, A * B * R
    HQ = W // (KV * H)
    KB = min(1024, FF)
    nc, nk = FF // CW, W // 1024
    nj, nd = W // CW, FF // KB
    direct = nc * nk * 2 + nj * nd <= SLOT_MAX
    node = lax.axis_index("node")
    tp = lax.axis_index("tp")
    a_me, b_me = lax.div(node, B), lax.rem(node, B)
    mine = b_me * A + a_me

    def outer(i):
        return lax.rem(a_me + i, A)

    def inner(i):
        return lax.rem(b_me + i, B)

    def dev(a, b):
        return {"node": a * B + b}

    def gu_copy(c, w, k):
        slot = (c * 2 + w) * nk + k
        src = gate_hbm if w == 0 else up_hbm
        col = pl.multiple_of(c * CW, CW)
        return pltpu.make_async_copy(
            src.at[pl.ds(k * 1024, 1024), pl.ds(col, CW)], wbuf.at[slot], wsem.at[slot]
        )

    def down_slot(j, k):
        return j * nd + k + (nc * nk * 2 if direct else 0)

    def down_copy(j, k):
        slot = down_slot(j, k)
        col = pl.multiple_of(j * CW, CW)
        return pltpu.make_async_copy(
            down_hbm.at[pl.ds(k * KB, KB), pl.ds(col, CW)],
            wbuf.at[slot, pl.ds(0, KB)],
            wsem.at[slot],
        )

    kcopy = pltpu.make_async_copy(ck_hbm, kbuf, cache_sem.at[0])
    vcopy = pltpu.make_async_copy(cv_hbm, vbuf, cache_sem.at[1])
    kcopy.start()
    vcopy.start()

    @pl.loop(0, nc)
    def _(c):
        for w in range(2):
            for k in range(nk):
                gu_copy(c, w, k).start()

    if direct:

        @pl.loop(0, nj)
        def _(j):
            for k in range(nd):
                down_copy(j, k).start()

    barrier = pltpu.get_barrier_semaphore()
    pl.semaphore_signal(
        barrier, inc=1, device_id={"tp": 1 - tp}, device_id_type=pl.DeviceIdType.MESH
    )
    for i in range(1, A):
        pl.semaphore_signal(
            barrier, inc=1, device_id=dev(outer(i), b_me), device_id_type=pl.DeviceIdType.MESH
        )
    for i in range(1, B):
        pl.semaphore_signal(
            barrier, inc=1, device_id=dev(a_me, inner(i)), device_id_type=pl.DeviceIdType.MESH
        )

    kcopy.wait()
    vcopy.wait()
    factor = 1.0 / math.sqrt(H)
    row128 = lax.broadcasted_iota(jnp.int32, (R, 128), 0)
    lenv = jnp.zeros((R, 128), jnp.int32)
    r0 = jnp.zeros((R, 128), jnp.int32)
    r1 = jnp.zeros((R, 128), jnp.int32)
    for r in range(R):
        lenv = jnp.where(row128 == r, lens_ref[r], lenv)
        r0 = jnp.where(row128 == r, routes_ref[0, r], r0)
        r1 = jnp.where(row128 == r, routes_ref[1, r], r1)
    col = lax.broadcasted_iota(jnp.int32, (R, R * L), 1)
    row = lax.broadcasted_iota(jnp.int32, (R, R * L), 0)
    valid = jnp.logical_and(col >= row * L, col < row * L + lenv[:, 0:1])
    bias = jnp.where(valid, 0.0, -jnp.inf).astype(F32)
    bias = jnp.concatenate([bias] * HQ, axis=0)
    square = jnp.zeros((R, 1), F32)
    logits = jnp.zeros((R, router_ref.shape[0]), F32)
    for g in range(KV):
        base = g * HQ * H
        q = jnp.concatenate([q_ref[:, base + h * H : base + (h + 1) * H] for h in range(HQ)], axis=0)
        keys = kbuf[:, g].reshape(R * L, H)
        values = vbuf[:, g].reshape(R * L, H)
        scores = lax.dot_general(q, keys, NT, preferred_element_type=F32) * factor + bias
        own_key = jnp.concatenate([nk_ref[:, g * H : (g + 1) * H].astype(F32)] * HQ, axis=0)
        own = jnp.sum(q.astype(F32) * own_key, axis=1, keepdims=True) * factor
        highest = jnp.maximum(jnp.max(scores, axis=1, keepdims=True), own)
        weights = jnp.exp(scores - highest)
        own_weight = jnp.exp(own - highest)
        total = jnp.sum(weights, axis=1, keepdims=True) + own_weight
        probs = (weights / total).astype(BF16)
        own_prob = (own_weight / total).astype(BF16).astype(F32)
        attended = jnp.dot(probs, values, preferred_element_type=F32)
        own_value = jnp.concatenate([nv_ref[:, g * H : (g + 1) * H].astype(F32)] * HQ, axis=0)
        attended = attended + own_prob * own_value
        for h in range(HQ):
            lo = base + h * H
            m = res_ref[:, lo : lo + H].astype(F32) + attended[h * R : (h + 1) * R]
            mixed[:, lo : lo + H] = m
            square = square + jnp.sum(m * m, axis=1, keepdims=True)
    gained = (mixed[...] * gain_ref[...]).astype(BF16)
    logits = lax.dot_general(gained, router_ref[...], NT, preferred_element_type=F32)
    stat_s[...] = jnp.zeros_like(stat_s)
    stat_s[:, 0:A] = logits
    stat_s[:, A : A + 1] = square

    pl.semaphore_wait(barrier, 1 + (A - 1) + (B - 1))
    stat_copy = pltpu.make_async_remote_copy(
        stat_s,
        stat_r,
        stat_sem.at[0],
        stat_sem.at[1],
        device_id={"tp": 1 - tp},
        device_id_type=pl.DeviceIdType.MESH,
    )
    stat_copy.start()
    stat_copy.wait()
    stat = stat_s[...] + stat_r[...]
    inverse = lax.rsqrt(stat[:, A : A + 1] / (2 * W) + 1e-05)
    logit = stat * inverse
    lane = lax.broadcasted_iota(jnp.int32, (R, 128), 1)
    p0 = jnp.sum(jnp.where(lane == r0, logit, 0.0), axis=1, keepdims=True)
    p1 = jnp.sum(jnp.where(lane == r1, logit, 0.0), axis=1, keepdims=True)
    w0 = 1.0 / (1.0 + jnp.exp(p1 - p0))
    w1 = 1.0 / (1.0 + jnp.exp(p0 - p1))
    pair = jnp.where(lane == r0, w0, 0.0) + jnp.where(lane == r1, w1, 0.0)
    pair_hi = pair.astype(BF16)
    lane_lo = lane - A
    low = jnp.where(lane_lo == r0, w0, 0.0) + jnp.where(lane_lo == r1, w1, 0.0)
    low = (low - low.astype(BF16).astype(F32)).astype(BF16)
    side_buf[mine] = pair_hi + low
    normed = (mixed[...] * inverse * gain_ref[...]).astype(BF16)
    for k in range(nk):
        xbuf[k, mine] = normed[:, k * 1024 : (k + 1) * 1024]

    def x_copy(k, block, sem, a, b):
        ref = side_buf.at[block] if k == nk else xbuf.at[k, block]
        return pltpu.make_async_remote_copy(
            ref,
            ref,
            sem,
            drecv_sem.at[k, block],
            device_id=dev(a, b),
            device_id_type=pl.DeviceIdType.MESH,
        )

    def pass_up(k, a):
        return x_copy(k, b_me * A + a, dsend_sem.at[k, 0, a], a_me + 1, b_me)

    def pass_down(k, a):
        return x_copy(k, b_me * A + a, dsend_sem.at[k, 1, a], a_me - 1, b_me)

    def relay(k, a, t):
        sem = rsend_sem.at[k, inner(t) * A + a]
        return x_copy(k, b_me * A + a, sem, a_me, inner(t))

    def arrival(k, a, t):
        return x_copy(k, inner(t) * A + a, dsend_sem.at[0, 0, 0], a_me, inner(1))

    def below_above(h):
        low_in = jnp.logical_and(a_me >= h, a_me < A - 1)
        high_in = jnp.logical_and(a_me + h < A, a_me > 0)
        return low_in, high_in

    parts = [nk] + list(range(nk))
    for k in parts:

        @pl.when(a_me < A - 1)
        def _():
            pass_up(k, a_me).start()

        @pl.when(a_me > 0)
        def _():
            pass_down(k, a_me).start()

        for t in range(1, B):
            relay(k, a_me, t).start()
    for h in range(1, A):
        low_in, high_in = below_above(h)
        for k in parts:

            @pl.when(a_me >= h)
            def _():
                arrival(k, a_me - h, 0).wait_recv()

            @pl.when(low_in)
            def _():
                pass_up(k, a_me - h).start()

            @pl.when(a_me + h < A)
            def _():
                arrival(k, a_me + h, 0).wait_recv()

            @pl.when(high_in)
            def _():
                pass_down(k, a_me + h).start()

            for t in range(1, B):

                @pl.when(a_me >= h)
                def _():
                    relay(k, a_me - h, t).start()

                @pl.when(a_me + h < A)
                def _():
                    relay(k, a_me + h, t).start()

    for k in parts:
        for t in range(1, B):
            for i in range(A):
                arrival(k, outer(i), t).wait_recv()

    def part_copy(c):
        s = lax.rem(c, 2)
        return pltpu.make_async_remote_copy(
            psend.at[s],
            precv.at[c],
            psend_sem.at[s],
            precv_sem.at[c],
            device_id={"tp": 1 - tp},
            device_id_type=pl.DeviceIdType.MESH,
        )

    def finish(c):
        s = lax.rem(c, 2)
        part_copy(c).wait_recv()
        gate = own_part[s, 0] + precv[c, 0].astype(F32)
        up = own_part[s, 1] + precv[c, 1].astype(F32)
        value = (gate / (1.0 + jnp.exp(-gate)) * up).astype(BF16)
        hidden[:, pl.ds(pl.multiple_of(c * CW, CW), CW)] = value

    @pl.loop(0, nc)
    def _(c):
        s = lax.rem(c, 2)

        @pl.when(c >= 2)
        def _():
            part_copy(c - 2).wait_send()

        for w in range(2):
            acc = None
            for k in range(nk):
                gu_copy(c, w, k).wait()
                lhs = xbuf[k].reshape(M, 1024)
                term = jnp.dot(lhs, wbuf[(c * 2 + w) * nk + k], preferred_element_type=F32)
                acc = term if acc is None else acc + term
            own_part[s, w] = acc
            psend[s, w] = acc.astype(BF16)
        part_copy(c).start()
        if not direct:
            per = 2 * nk // nd if (2 * nk) % nd == 0 else 1

            @pl.when(c * per < nj)
            def _():
                for p in range(per):

                    @pl.when(c * per + p < nj)
                    def _():
                        for k in range(nd):
                            down_copy(c * per + p, k).start()

        @pl.when(c >= 1)
        def _():
            finish(c - 1)

    finish(nc - 1)
    for c in range(max(0, nc - 2), nc):
        part_copy(c).wait_send()

    side = side_buf[...].reshape(M, 128).astype(F32)
    lane_m = lax.broadcasted_iota(jnp.int32, (M, 128), 1)
    keep = jnp.logical_or(lane_m == a_me, lane_m == a_me + A)
    pairw = jnp.sum(jnp.where(keep, side, 0.0), axis=1, keepdims=True)

    G = A * R

    def xs_copy(j, t):
        other = inner(t)
        return pltpu.make_async_remote_copy(
            xsend.at[j, other],
            xrecv.at[j, b_me],
            xsend_sem.at[j, other],
            xrecv_sem.at[j, b_me],
            device_id=dev(a_me, other),
            device_id_type=pl.DeviceIdType.MESH,
        )

    def xs_arrival(j, t):
        other = inner(t)
        return pltpu.make_async_remote_copy(
            xsend.at[j, b_me],
            xrecv.at[j, other],
            xsend_sem.at[j, b_me],
            xrecv_sem.at[j, other],
            device_id=dev(a_me, other),
            device_id_type=pl.DeviceIdType.MESH,
        )

    def zs_copy(j, i):
        other = outer(i)
        return pltpu.make_async_remote_copy(
            zsend.at[j, other],
            zrecv.at[j, a_me],
            zsend_sem.at[j, other],
            zrecv_sem.at[j, a_me],
            device_id=dev(other, b_me),
            device_id_type=pl.DeviceIdType.MESH,
        )

    def zs_arrival(j, i):
        other = outer(i)
        return pltpu.make_async_remote_copy(
            zsend.at[j, a_me],
            zrecv.at[j, other],
            zsend_sem.at[j, a_me],
            zrecv_sem.at[j, other],
            device_id=dev(other, b_me),
            device_id_type=pl.DeviceIdType.MESH,
        )

    def stage_one(j):
        acc = None
        for k in range(nd):
            down_copy(j, k).wait()
            term = jnp.dot(
                hidden[:, k * KB : (k + 1) * KB],
                wbuf[down_slot(j, k), 0:KB],
                preferred_element_type=F32,
            )
            acc = term if acc is None else acc + term
        acc = acc * pairw
        for b in range(B):
            xsend[j, b] = acc[b * G : (b + 1) * G].astype(BF16)
            mask = jnp.where(b_me == b, 1.0, 0.0)
            if b == 0:
                kept = acc[0:G] * mask
            else:
                kept = kept + acc[b * G : (b + 1) * G] * mask
        xown[lax.rem(j, 2)] = kept
        for t in range(1, B):
            xs_copy(j, t).start()

    def stage_two(j):
        total = xown[lax.rem(j, 2)]
        for t in range(1, B):
            xs_arrival(j, t).wait_recv()
            total = total + xrecv[j, inner(t)].astype(F32)
        zown[j] = total
        for a in range(A):
            zsend[j, a] = total[a * R : (a + 1) * R].astype(BF16)
        for i in range(1, A):
            zs_copy(j, i).start()

    def stage_three(j):
        cols = pl.ds(pl.multiple_of(j * CW, CW), CW)
        total = mixed[:, cols] + zown[j, pl.ds(pl.multiple_of(a_me * R, R), R), :]
        for i in range(1, A):
            zs_arrival(j, i).wait_recv()
            total = total + zrecv[j, outer(i)].astype(F32)
        out_ref[:, cols] = total.astype(BF16)

    @pl.loop(0, nj)
    def _(j):
        stage_one(j)

        @pl.when(j >= 1)
        def _():
            stage_two(j - 1)

        @pl.when(j >= 2)
        def _():
            stage_three(j - 2)

    stage_two(nj - 1)
    stage_three(nj - 2)
    stage_three(nj - 1)

    for k in parts:
        for h in range(A):
            low_in, high_in = below_above(h)

            @pl.when(low_in)
            def _():
                pass_up(k, a_me - h).wait_send()

            @pl.when(high_in)
            def _():
                pass_down(k, a_me + h).wait_send()

        for t in range(1, B):
            for i in range(A):
                relay(k, outer(i), t).wait_send()

    @pl.loop(0, nj)
    def _(j):
        for t in range(1, B):
            xs_copy(j, t).wait_send()
        for i in range(1, A):
            zs_copy(j, i).wait_send()


def local(
    residual,
    queries,
    new_keys,
    new_values,
    cache_keys,
    cache_values,
    lengths,
    routes,
    norm_gain,
    router_weight,
    gate_weight,
    up_weight,
    down_weight,
):
    R, W = residual.shape
    FF = gate_weight.shape[1]
    _, KV, L, H = cache_keys.shape
    A = router_weight.shape[1]
    B = lax.axis_size("node") // A
    N, M = A * B, A * B * R
    KB = min(1024, FF)
    nc, nk, nj, nd = FF // CW, W // 1024, W // CW, FF // KB
    gu = nc * nk * 2
    slots = gu + nj * nd if gu + nj * nd <= SLOT_MAX else gu
    cfg = (A, B, R, W, FF, KV, L, H)
    vmem = pl.BlockSpec(memory_space=pltpu.VMEM)
    smem = pl.BlockSpec(memory_space=pltpu.SMEM)
    hbm = pl.BlockSpec(memory_space=pl.ANY)
    dma = pltpu.SemaphoreType.DMA
    return pl.pallas_call(
        functools.partial(layer_kernel, cfg),
        out_shape=jax.ShapeDtypeStruct((R, W), BF16),
        in_specs=[smem, smem, vmem, vmem, vmem, vmem, hbm, hbm, vmem, vmem, hbm, hbm, hbm],
        out_specs=vmem,
        scratch_shapes=[
            pltpu.VMEM((R, KV, L, H), BF16),
            pltpu.VMEM((R, KV, L, H), BF16),
            pltpu.VMEM((slots, 1024, CW), BF16),
            pltpu.VMEM((nk, N, R, 1024), BF16),
            pltpu.VMEM((N, R, 128), BF16),
            pltpu.VMEM((R, W), F32),
            pltpu.VMEM((R, 128), F32),
            pltpu.VMEM((R, 128), F32),
            pltpu.VMEM((2, 2, M, CW), F32),
            pltpu.VMEM((2, 2, M, CW), BF16),
            pltpu.VMEM((nc, 2, M, CW), BF16),
            pltpu.VMEM((M, FF), BF16),
            pltpu.VMEM((nj, B, A * R, CW), BF16),
            pltpu.VMEM((nj, B, A * R, CW), BF16),
            pltpu.VMEM((2, A * R, CW), F32),
            pltpu.VMEM((nj, A, R, CW), BF16),
            pltpu.VMEM((nj, A, R, CW), BF16),
            pltpu.VMEM((nj, A * R, CW), F32),
            dma((2,)),
            dma((slots,)),
            dma((2,)),
            dma((nk + 1, 2, A)),
            dma((nk + 1, N)),
            dma((nk + 1, N)),
            dma((2,)),
            dma((nc,)),
            dma((nj, B)),
            dma((nj, B)),
            dma((nj, A)),
            dma((nj, A)),
        ],
        compiler_params=pltpu.CompilerParams(
            collective_id=0, has_side_effects=True, vmem_limit_bytes=63 * 1024 * 1024
        ),
    )(
        lengths,
        routes.T,
        residual,
        queries,
        new_keys,
        new_values,
        cache_keys,
        cache_values,
        norm_gain.reshape(1, -1),
        router_weight.T,
        gate_weight,
        up_weight,
        down_weight,
    )


def solution(mesh):
    placed = (
        P(("group", "node"), "tp"),
        P(("group", "node"), "tp"),
        P(("group", "node"), "tp"),
        P(("group", "node"), "tp"),
        P(("group", "node"), "tp", None, None),
        P(("group", "node"), "tp", None, None),
        P(("group", "node")),
        P(("group", "node"), None),
        P("tp"),
        P("tp", None),
        P("tp", "node"),
        P("tp", "node"),
        P("node", "tp"),
    )
    return jax.shard_map(
        local, mesh=mesh, in_specs=placed, out_specs=P(("group", "node"), "tp"), check_vma=False
    )
```

```python
import functools
import math

import jax
import jax.numpy as jnp
from jax import lax
from jax.experimental import pallas as pl
from jax.experimental.pallas import tpu as pltpu
from jax.sharding import PartitionSpec as P

F32, BF16 = jnp.float32, jnp.bfloat16
NT = (((1,), (1,)), ((), ()))
SLOT_MAX = 48
CW = 512


def layer_kernel(
    cfg,
    lens_ref,
    routes_ref,
    res_ref,
    q_ref,
    nk_ref,
    nv_ref,
    ck_hbm,
    cv_hbm,
    gain_ref,
    router_ref,
    gate_hbm,
    up_hbm,
    down_hbm,
    out_ref,
    kbuf,
    vbuf,
    wbuf,
    xbuf,
    side_buf,
    mixed,
    stat_s,
    stat_r,
    own_part,
    psend,
    precv,
    hidden,
    xsend,
    xrecv,
    xown,
    zsend,
    zrecv,
    zown,
    cache_sem,
    wsem,
    stat_sem,
    dsend_sem,
    rsend_sem,
    drecv_sem,
    psend_sem,
    precv_sem,
    xsend_sem,
    xrecv_sem,
    zsend_sem,
    zrecv_sem,
):
    A, B, R, W, FF, KV, L, H = cfg
    N, M = A * B, A * B * R
    HQ = W // (KV * H)
    KB = min(1024, FF)
    nc, nk = FF // CW, W // 1024
    nj, nd = W // CW, FF // KB
    direct = nc * nk * 2 + nj * nd <= SLOT_MAX
    node = lax.axis_index("node")
    tp = lax.axis_index("tp")
    a_me, b_me = lax.div(node, B), lax.rem(node, B)
    mine = b_me * A + a_me

    def outer(i):
        return lax.rem(a_me + i, A)

    def inner(i):
        return lax.rem(b_me + i, B)

    def dev(a, b):
        return {"node": a * B + b}

    def gu_copy(c, w, k):
        slot = (c * 2 + w) * nk + k
        src = gate_hbm if w == 0 else up_hbm
        col = pl.multiple_of(c * CW, CW)
        return pltpu.make_async_copy(
            src.at[pl.ds(k * 1024, 1024), pl.ds(col, CW)], wbuf.at[slot], wsem.at[slot]
        )

    def down_slot(j, k):
        return j * nd + k + (nc * nk * 2 if direct else 0)

    def down_copy(j, k):
        slot = down_slot(j, k)
        col = pl.multiple_of(j * CW, CW)
        return pltpu.make_async_copy(
            down_hbm.at[pl.ds(k * KB, KB), pl.ds(col, CW)],
            wbuf.at[slot, pl.ds(0, KB)],
            wsem.at[slot],
        )

    kcopy = pltpu.make_async_copy(ck_hbm, kbuf, cache_sem.at[0])
    vcopy = pltpu.make_async_copy(cv_hbm, vbuf, cache_sem.at[1])
    kcopy.start()
    vcopy.start()

    @pl.loop(0, nc)
    def _(c):
        for w in range(2):
            for k in range(nk):
                gu_copy(c, w, k).start()

    if direct:

        @pl.loop(0, nj)
        def _(j):
            for k in range(nd):
                down_copy(j, k).start()

    barrier = pltpu.get_barrier_semaphore()
    pl.semaphore_signal(
        barrier, inc=1, device_id={"tp": 1 - tp}, device_id_type=pl.DeviceIdType.MESH
    )
    for i in range(1, A):
        pl.semaphore_signal(
            barrier, inc=1, device_id=dev(outer(i), b_me), device_id_type=pl.DeviceIdType.MESH
        )
    for i in range(1, B):
        pl.semaphore_signal(
            barrier, inc=1, device_id=dev(a_me, inner(i)), device_id_type=pl.DeviceIdType.MESH
        )

    kcopy.wait()
    vcopy.wait()
    factor = 1.0 / math.sqrt(H)
    row128 = lax.broadcasted_iota(jnp.int32, (R, 128), 0)
    lenv = jnp.zeros((R, 128), jnp.int32)
    r0 = jnp.zeros((R, 128), jnp.int32)
    r1 = jnp.zeros((R, 128), jnp.int32)
    for r in range(R):
        lenv = jnp.where(row128 == r, lens_ref[r], lenv)
        r0 = jnp.where(row128 == r, routes_ref[0, r], r0)
        r1 = jnp.where(row128 == r, routes_ref[1, r], r1)
    col = lax.broadcasted_iota(jnp.int32, (R, R * L), 1)
    row = lax.broadcasted_iota(jnp.int32, (R, R * L), 0)
    valid = jnp.logical_and(col >= row * L, col < row * L + lenv[:, 0:1])
    bias = jnp.where(valid, 0.0, -jnp.inf).astype(F32)
    bias = jnp.concatenate([bias] * HQ, axis=0)
    square = jnp.zeros((R, 1), F32)
    logits = jnp.zeros((R, router_ref.shape[0]), F32)
    for g in range(KV):
        base = g * HQ * H
        q = jnp.concatenate([q_ref[:, base + h * H : base + (h + 1) * H] for h in range(HQ)], axis=0)
        keys = kbuf[:, g].reshape(R * L, H)
        values = vbuf[:, g].reshape(R * L, H)
        scores = lax.dot_general(q, keys, NT, preferred_element_type=F32) * factor + bias
        own_key = jnp.concatenate([nk_ref[:, g * H : (g + 1) * H].astype(F32)] * HQ, axis=0)
        own = jnp.sum(q.astype(F32) * own_key, axis=1, keepdims=True) * factor
        highest = jnp.maximum(jnp.max(scores, axis=1, keepdims=True), own)
        weights = jnp.exp(scores - highest)
        own_weight = jnp.exp(own - highest)
        total = jnp.sum(weights, axis=1, keepdims=True) + own_weight
        probs = (weights / total).astype(BF16)
        own_prob = (own_weight / total).astype(BF16).astype(F32)
        attended = jnp.dot(probs, values, preferred_element_type=F32)
        own_value = jnp.concatenate([nv_ref[:, g * H : (g + 1) * H].astype(F32)] * HQ, axis=0)
        attended = attended + own_prob * own_value
        for h in range(HQ):
            lo = base + h * H
            m = res_ref[:, lo : lo + H].astype(F32) + attended[h * R : (h + 1) * R]
            mixed[:, lo : lo + H] = m
            square = square + jnp.sum(m * m, axis=1, keepdims=True)
    gained = (mixed[...] * gain_ref[...]).astype(BF16)
    logits = lax.dot_general(gained, router_ref[...], NT, preferred_element_type=F32)
    stat_s[...] = jnp.zeros_like(stat_s)
    stat_s[:, 0:A] = logits
    stat_s[:, A : A + 1] = square

    pl.semaphore_wait(barrier, 1 + (A - 1) + (B - 1))
    stat_copy = pltpu.make_async_remote_copy(
        stat_s,
        stat_r,
        stat_sem.at[0],
        stat_sem.at[1],
        device_id={"tp": 1 - tp},
        device_id_type=pl.DeviceIdType.MESH,
    )
    stat_copy.start()
    stat_copy.wait()
    stat = stat_s[...] + stat_r[...]
    inverse = lax.rsqrt(stat[:, A : A + 1] / (2 * W) + 1e-05)
    logit = stat * inverse
    lane = lax.broadcasted_iota(jnp.int32, (R, 128), 1)
    p0 = jnp.sum(jnp.where(lane == r0, logit, 0.0), axis=1, keepdims=True)
    p1 = jnp.sum(jnp.where(lane == r1, logit, 0.0), axis=1, keepdims=True)
    w0 = 1.0 / (1.0 + jnp.exp(p1 - p0))
    w1 = 1.0 / (1.0 + jnp.exp(p0 - p1))
    pair = jnp.where(lane == r0, w0, 0.0) + jnp.where(lane == r1, w1, 0.0)
    pair_hi = pair.astype(BF16)
    lane_lo = lane - A
    low = jnp.where(lane_lo == r0, w0, 0.0) + jnp.where(lane_lo == r1, w1, 0.0)
    low = (low - low.astype(BF16).astype(F32)).astype(BF16)
    side_buf[mine] = pair_hi + low
    normed = (mixed[...] * inverse * gain_ref[...]).astype(BF16)
    for k in range(nk):
        xbuf[k, mine] = normed[:, k * 1024 : (k + 1) * 1024]

    def x_copy(k, block, sem, a, b):
        ref = side_buf.at[block] if k == nk else xbuf.at[k, block]
        return pltpu.make_async_remote_copy(
            ref,
            ref,
            sem,
            drecv_sem.at[k, block],
            device_id=dev(a, b),
            device_id_type=pl.DeviceIdType.MESH,
        )

    def pass_up(k, a):
        return x_copy(k, b_me * A + a, dsend_sem.at[k, 0, a], a_me + 1, b_me)

    def pass_down(k, a):
        return x_copy(k, b_me * A + a, dsend_sem.at[k, 1, a], a_me - 1, b_me)

    def relay(k, a, t):
        sem = rsend_sem.at[k, inner(t) * A + a]
        return x_copy(k, b_me * A + a, sem, a_me, inner(t))

    def arrival(k, a, t):
        return x_copy(k, inner(t) * A + a, dsend_sem.at[0, 0, 0], a_me, inner(1))

    def below_above(h):
        low_in = jnp.logical_and(a_me >= h, a_me < A - 1)
        high_in = jnp.logical_and(a_me + h < A, a_me > 0)
        return low_in, high_in

    parts = [nk] + list(range(nk))
    for k in parts:

        @pl.when(a_me < A - 1)
        def _():
            pass_up(k, a_me).start()

        @pl.when(a_me > 0)
        def _():
            pass_down(k, a_me).start()

        for t in range(1, B):
            relay(k, a_me, t).start()
    for h in range(1, A):
        low_in, high_in = below_above(h)
        for k in parts:

            @pl.when(a_me >= h)
            def _():
                arrival(k, a_me - h, 0).wait_recv()

            @pl.when(low_in)
            def _():
                pass_up(k, a_me - h).start()

            @pl.when(a_me + h < A)
            def _():
                arrival(k, a_me + h, 0).wait_recv()

            @pl.when(high_in)
            def _():
                pass_down(k, a_me + h).start()

            for t in range(1, B):

                @pl.when(a_me >= h)
                def _():
                    relay(k, a_me - h, t).start()

                @pl.when(a_me + h < A)
                def _():
                    relay(k, a_me + h, t).start()

    for k in parts:
        for t in range(1, B):
            for i in range(A):
                arrival(k, outer(i), t).wait_recv()

    def part_copy(c):
        s = lax.rem(c, 2)
        return pltpu.make_async_remote_copy(
            psend.at[s],
            precv.at[c],
            psend_sem.at[s],
            precv_sem.at[c],
            device_id={"tp": 1 - tp},
            device_id_type=pl.DeviceIdType.MESH,
        )

    def finish(c):
        s = lax.rem(c, 2)
        part_copy(c).wait_recv()
        gate = own_part[s, 0] + precv[c, 0].astype(F32)
        up = own_part[s, 1] + precv[c, 1].astype(F32)
        value = (gate / (1.0 + jnp.exp(-gate)) * up).astype(BF16)
        hidden[:, pl.ds(pl.multiple_of(c * CW, CW), CW)] = value

    @pl.loop(0, nc)
    def _(c):
        s = lax.rem(c, 2)

        @pl.when(c >= 2)
        def _():
            part_copy(c - 2).wait_send()

        for w in range(2):
            acc = None
            for k in range(nk):
                gu_copy(c, w, k).wait()
                lhs = xbuf[k].reshape(M, 1024)
                term = jnp.dot(lhs, wbuf[(c * 2 + w) * nk + k], preferred_element_type=F32)
                acc = term if acc is None else acc + term
            own_part[s, w] = acc
            psend[s, w] = acc.astype(BF16)
        part_copy(c).start()
        if not direct:
            per = 2 * nk // nd if (2 * nk) % nd == 0 else 1

            @pl.when(c * per < nj)
            def _():
                for p in range(per):

                    @pl.when(c * per + p < nj)
                    def _():
                        for k in range(nd):
                            down_copy(c * per + p, k).start()

        @pl.when(c >= 1)
        def _():
            finish(c - 1)

    finish(nc - 1)
    for c in range(max(0, nc - 2), nc):
        part_copy(c).wait_send()

    side = side_buf[...].reshape(M, 128).astype(F32)
    lane_m = lax.broadcasted_iota(jnp.int32, (M, 128), 1)
    keep = jnp.logical_or(lane_m == a_me, lane_m == a_me + A)
    pairw = jnp.sum(jnp.where(keep, side, 0.0), axis=1, keepdims=True)

    G = A * R

    def xs_copy(j, t):
        other = inner(t)
        return pltpu.make_async_remote_copy(
            xsend.at[j, other],
            xrecv.at[j, b_me],
            xsend_sem.at[j, other],
            xrecv_sem.at[j, b_me],
            device_id=dev(a_me, other),
            device_id_type=pl.DeviceIdType.MESH,
        )

    def xs_arrival(j, t):
        other = inner(t)
        return pltpu.make_async_remote_copy(
            xsend.at[j, b_me],
            xrecv.at[j, other],
            xsend_sem.at[j, b_me],
            xrecv_sem.at[j, other],
            device_id=dev(a_me, other),
            device_id_type=pl.DeviceIdType.MESH,
        )

    def zs_copy(j, i):
        other = outer(i)
        return pltpu.make_async_remote_copy(
            zsend.at[j, other],
            zrecv.at[j, a_me],
            zsend_sem.at[j, other],
            zrecv_sem.at[j, a_me],
            device_id=dev(other, b_me),
            device_id_type=pl.DeviceIdType.MESH,
        )

    def zs_arrival(j, i):
        other = outer(i)
        return pltpu.make_async_remote_copy(
            zsend.at[j, a_me],
            zrecv.at[j, other],
            zsend_sem.at[j, a_me],
            zrecv_sem.at[j, other],
            device_id=dev(other, b_me),
            device_id_type=pl.DeviceIdType.MESH,
        )

    def stage_one(j):
        acc = None
        for k in range(nd):
            down_copy(j, k).wait()
            term = jnp.dot(
                hidden[:, k * KB : (k + 1) * KB],
                wbuf[down_slot(j, k), 0:KB],
                preferred_element_type=F32,
            )
            acc = term if acc is None else acc + term
        acc = acc * pairw
        for b in range(B):
            xsend[j, b] = acc[b * G : (b + 1) * G].astype(BF16)
            mask = jnp.where(b_me == b, 1.0, 0.0)
            if b == 0:
                kept = acc[0:G] * mask
            else:
                kept = kept + acc[b * G : (b + 1) * G] * mask
        xown[lax.rem(j, 3)] = kept
        for t in range(1, B):
            xs_copy(j, t).start()

    def stage_two(j):
        total = xown[lax.rem(j, 3)]
        for t in range(1, B):
            xs_arrival(j, t).wait_recv()
            total = total + xrecv[j, inner(t)].astype(F32)
        zown[j] = total
        for a in range(A):
            zsend[j, a] = total[a * R : (a + 1) * R].astype(BF16)
        for i in range(1, A):
            zs_copy(j, i).start()

    def stage_three(j):
        cols = pl.ds(pl.multiple_of(j * CW, CW), CW)
        total = mixed[:, cols] + zown[j, pl.ds(pl.multiple_of(a_me * R, R), R), :]
        for i in range(1, A):
            zs_arrival(j, i).wait_recv()
            total = total + zrecv[j, outer(i)].astype(F32)
        out_ref[:, cols] = total.astype(BF16)

    @pl.loop(0, nj)
    def _(j):
        stage_one(j)

        @pl.when(j >= 2)
        def _():
            stage_two(j - 2)

    stage_two(nj - 2)
    stage_two(nj - 1)

    @pl.loop(0, nj)
    def _(j):
        stage_three(j)

    for k in parts:
        for h in range(A):
            low_in, high_in = below_above(h)

            @pl.when(low_in)
            def _():
                pass_up(k, a_me - h).wait_send()

            @pl.when(high_in)
            def _():
                pass_down(k, a_me + h).wait_send()

        for t in range(1, B):
            for i in range(A):
                relay(k, outer(i), t).wait_send()

    @pl.loop(0, nj)
    def _(j):
        for t in range(1, B):
            xs_copy(j, t).wait_send()
        for i in range(1, A):
            zs_copy(j, i).wait_send()


def local(
    residual,
    queries,
    new_keys,
    new_values,
    cache_keys,
    cache_values,
    lengths,
    routes,
    norm_gain,
    router_weight,
    gate_weight,
    up_weight,
    down_weight,
):
    R, W = residual.shape
    FF = gate_weight.shape[1]
    _, KV, L, H = cache_keys.shape
    A = router_weight.shape[1]
    B = lax.axis_size("node") // A
    N, M = A * B, A * B * R
    KB = min(1024, FF)
    nc, nk, nj, nd = FF // CW, W // 1024, W // CW, FF // KB
    gu = nc * nk * 2
    slots = gu + nj * nd if gu + nj * nd <= SLOT_MAX else gu
    cfg = (A, B, R, W, FF, KV, L, H)
    vmem = pl.BlockSpec(memory_space=pltpu.VMEM)
    smem = pl.BlockSpec(memory_space=pltpu.SMEM)
    hbm = pl.BlockSpec(memory_space=pl.ANY)
    dma = pltpu.SemaphoreType.DMA
    return pl.pallas_call(
        functools.partial(layer_kernel, cfg),
        out_shape=jax.ShapeDtypeStruct((R, W), BF16),
        in_specs=[smem, smem, vmem, vmem, vmem, vmem, hbm, hbm, vmem, vmem, hbm, hbm, hbm],
        out_specs=vmem,
        scratch_shapes=[
            pltpu.VMEM((R, KV, L, H), BF16),
            pltpu.VMEM((R, KV, L, H), BF16),
            pltpu.VMEM((slots, 1024, CW), BF16),
            pltpu.VMEM((nk, N, R, 1024), BF16),
            pltpu.VMEM((N, R, 128), BF16),
            pltpu.VMEM((R, W), F32),
            pltpu.VMEM((R, 128), F32),
            pltpu.VMEM((R, 128), F32),
            pltpu.VMEM((2, 2, M, CW), F32),
            pltpu.VMEM((2, 2, M, CW), BF16),
            pltpu.VMEM((nc, 2, M, CW), BF16),
            pltpu.VMEM((M, FF), BF16),
            pltpu.VMEM((nj, B, A * R, CW), BF16),
            pltpu.VMEM((nj, B, A * R, CW), BF16),
            pltpu.VMEM((3, A * R, CW), F32),
            pltpu.VMEM((nj, A, R, CW), BF16),
            pltpu.VMEM((nj, A, R, CW), BF16),
            pltpu.VMEM((nj, A * R, CW), F32),
            dma((2,)),
            dma((slots,)),
            dma((2,)),
            dma((nk + 1, 2, A)),
            dma((nk + 1, N)),
            dma((nk + 1, N)),
            dma((2,)),
            dma((nc,)),
            dma((nj, B)),
            dma((nj, B)),
            dma((nj, A)),
            dma((nj, A)),
        ],
        compiler_params=pltpu.CompilerParams(
            collective_id=0, has_side_effects=True, vmem_limit_bytes=63 * 1024 * 1024
        ),
    )(
        lengths,
        routes.T,
        residual,
        queries,
        new_keys,
        new_values,
        cache_keys,
        cache_values,
        norm_gain.reshape(1, -1),
        router_weight.T,
        gate_weight,
        up_weight,
        down_weight,
    )


def solution(mesh):
    placed = (
        P(("group", "node"), "tp"),
        P(("group", "node"), "tp"),
        P(("group", "node"), "tp"),
        P(("group", "node"), "tp"),
        P(("group", "node"), "tp", None, None),
        P(("group", "node"), "tp", None, None),
        P(("group", "node")),
        P(("group", "node"), None),
        P("tp"),
        P("tp", None),
        P("tp", "node"),
        P("tp", "node"),
        P("node", "tp"),
    )
    return jax.shard_map(
        local, mesh=mesh, in_specs=placed, out_specs=P(("group", "node"), "tp"), check_vma=False
    )
```
